32 devices in a mesh: dp: 4 (over x, core), tm: 8 (over z, y).
Axes of the slice: x: 2, y: 2, z: 4, core: 2. Of those that a mesh axis runs over, the one named last changes fastest.
Arguments:
- tokens: bfloat16 [4, 8, 512, 768], P('dp', 'tm'), may hold values from -60 to 60
- qkv_weight: bfloat16 [768, 2304], replicated, may hold values from -0.21875 to 0.21875
- pool_kernel: float32 [2, 27, 64], replicated, may hold values from -1.25 to 1.25
- norm_gain: float32 [2, 64], replicated, may hold values from 0.1 to 1.9
- out_weight: bfloat16 [768, 768], replicated, may hold values from -0.21875 to 0.21875
- out_cotangent: bfloat16 [4, 8, 512, 768], P('dp', 'tm'), may hold values from -6 to 6
Outputs:
- block_out: bfloat16 [4, 8, 512, 768], P('dp', 'tm')
- grad_tokens: bfloat16 [4, 8, 512, 768], P('dp', 'tm')
- grad_qkv_weight: float32 [768, 2304], P('tm')
- grad_out_weight: float32 [768, 768], P('tm')
- grad_kernel: float32 [2, 27, 64], replicated
- grad_gain: float32 [2, 64], replicated
The draws below stay inside these ranges and needn't reach their ends.
All inputs are finite; a program needn't handle non-finite values.
Results may differ from the reference program's by a relative error of at most 0.0055.
The reference program's roundings to bfloat16 on the way (of `projected`, `pooled`, `weights`, `mixed`, `d_mixed`, `scaled_grad`, `d_scores` and `d_projected`) count: a program that leaves them out, or rounds other values in their place, can miss the bound.
Values may be sent and summed in bfloat16 or wider, within the bound.
A program may use at most 128 MiB of HBM per device.

```python
import math
from functools import partial
import jax
import jax.numpy as jnp
from jax import lax

D = 768
HEADS = 12
GRID_H = 32
GRID_W = 16
HEAD_DIM = 64
HW = 512
FRAMES = 8
CLIPS = 4
TOKENS = 16384


def draw_tokens(key, part):
    keys_split = jax.random.split(key, 3)
    extent = (CLIPS, FRAMES, HW, D)
    base = jax.random.normal(keys_split[0], extent, jnp.float32)
    token_scale = jnp.exp(jax.random.uniform(keys_split[1], extent[:3] + (1,), jnp.float32, 0.0, math.log(10.0)))
    channel_scale = jnp.exp(jax.random.uniform(keys_split[2], (D,), jnp.float32, math.log(0.5), math.log(2.0)))
    values = jnp.clip(0.5 * base * token_scale * channel_scale, -60.0, 60.0)
    return values.astype(jnp.bfloat16)


def shard_levels(rng, shape, cuts, smallest, high):
    loudness = 1.0
    for dim, parts in cuts:
        heights = jax.random.uniform(jax.random.fold_in(jax.random.fold_in(rng, 6), dim), (parts,), jnp.float32, smallest / len(cuts), high / len(cuts))
        loudness = loudness * jnp.repeat(jnp.exp(heights), shape[dim] // parts).reshape((-1,) + (1,) * (len(shape) - 1 - dim))
    return loudness


def bell_draw(stream_key, shape, spread, reach, cuts=(), kind=jnp.bfloat16):
    values = jax.random.normal(stream_key, shape, jnp.float32) * spread
    if len(cuts) > 0:
        values = shard_levels(stream_key, shape, cuts, -0.22, 0.18) * values
    return jnp.clip(values, min=-reach, max=reach).astype(kind)


def setup_inputs(seed: int = 0) -> dict:
    key_list = jax.random.split(jax.random.key(seed), 7)
    return {
        "tokens": draw_tokens(jax.random.fold_in(key_list[6], 71), 0),
        "qkv_weight": bell_draw(key_list[1], (D, 3 * D), D ** -0.5, 0.21875),
        "pool_kernel": bell_draw(key_list[2], (2, 27, HEAD_DIM), 27 ** -0.5, 1.25, (), jnp.float32),
        "norm_gain": jnp.clip(1.0 + 0.18 * jax.random.normal(key_list[3], (2, HEAD_DIM), jnp.float32), 0.1, 1.9),
        "out_weight": bell_draw(key_list[4], (D, D), D ** -0.5, 0.21875),
        "out_cotangent": bell_draw(key_list[5], (CLIPS, FRAMES, HW, D), 1.0, 6.0, ((0, 4), (1, 8))),
    }


EPSILON = 1e-05
pair_heads = 2

def exact_einsum(formula, first_operand, second_operand):
    return jnp.einsum(formula, first_operand.astype(jnp.float32), second_operand.astype(jnp.float32), precision=lax.Precision.HIGHEST)

def tap_table(kernel, head_count):
    tiled = jnp.tile(kernel, (1, 1, head_count))
    return jnp.transpose(tiled, (1, 0, 2)).reshape(3, 3, 3, -1)

def cut_blocks(volume):
    lead_dims = volume.ndim - 3
    extent = volume.shape
    padded = jnp.pad(volume, [(0, 0)] * lead_dims + [(1, 3), (1, 3), (0, 0)])
    pooled_h = extent[-3] // 4
    pooled_w = extent[-2] // 4
    tiled_view = padded.reshape(extent[:-3] + (pooled_h + 1, 4, pooled_w + 1, 4, extent[-1]))
    return tiled_view[..., :pooled_h, :3, :pooled_w, :3, :]

def spatial_sums(blocks, kernel_taps):
    widened = blocks.astype(jnp.float32)
    results = []
    for offset_t in range(3):
        running = None
        for offset_h in range(3):
            for offset_w in range(3):
                product_term = widened[..., offset_h, :, offset_w, :] * kernel_taps[offset_t, offset_h, offset_w]
                running = product_term if running is None else running + product_term
        results.append(running)
    return results

def spread_taps(shifted, kernel_taps, height, breadth):
    running = None
    for offset_t in range(3):
        product_term = shifted[offset_t][..., :, None, :, None, :] * kernel_taps[offset_t][:, None, :, :]
        running = product_term if running is None else running + product_term
    lead_dims = running.ndim - 5
    padded = jnp.pad(running, [(0, 0)] * lead_dims + [(0, 1)] * 4 + [(0, 0)])
    extent = padded.shape
    volume = padded.reshape(extent[:lead_dims] + (extent[lead_dims] * 4, extent[lead_dims + 2] * 4, extent[-1]))
    return volume[..., 1:height + 1, 1:breadth + 1, :]

def tap_grads(shifted, blocks, head_count):
    widened = blocks.astype(jnp.float32)
    per_offset = [jnp.einsum('cfijd,cfibjed->bed', shifted[offset_t], widened, precision=lax.Precision.HIGHEST) for offset_t in range(3)]
    stacked = jnp.stack(per_offset).reshape(27, 2, head_count, -1)
    return jnp.transpose(lax.optimization_barrier(jnp.sum(stacked, axis=2)), (1, 0, 2))

def pooled_norm(summed, gain, head_count):
    grouped_view = summed.reshape(summed.shape[:-1] + (2, head_count, -1))
    centred = grouped_view - lax.optimization_barrier(jnp.mean(grouped_view, axis=-1, keepdims=True))
    inv_std = lax.rsqrt(lax.optimization_barrier(jnp.mean(centred * centred, axis=-1, keepdims=True)) + EPSILON)
    normed = centred * inv_std
    pooled = (normed * gain[:, None, :]).reshape(summed.shape).astype(jnp.bfloat16)
    return (pooled, normed, inv_std)

def split_heads(tensor):
    extent = tensor.shape
    paired = tensor.reshape(extent[:2] + (extent[2] // pair_heads, pair_heads) + extent[3:])
    return jnp.moveaxis(paired, 2, 0)

def join_heads(tensor):
    moved = jnp.moveaxis(tensor, 0, 2)
    extent = moved.shape
    return moved.reshape(extent[:2] + (extent[2] * extent[3],) + extent[4:])

def by_pairs(function, tensors):
    results = lax.map(lambda members: function(*members), tuple((split_heads(element) for element in tensors)))
    return tuple((join_heads(element) for element in results))

def group_forward(queries, keys_part, values_part, softmax_scale):
    scores = exact_einsum('crgd,ckgd->crgk', queries, keys_part) * softmax_scale
    row_max = lax.optimization_barrier(jnp.max(scores, axis=-1))
    weights = jnp.exp(scores - row_max[..., None])
    row_total = lax.optimization_barrier(jnp.sum(weights, axis=-1))
    weighted = exact_einsum('crgk,ckgd->crgd', weights.astype(jnp.bfloat16), values_part)
    return (row_max, row_total, weighted)

def group_backward(queries, keys_part, values_part, row_max, row_total, attended, d_mixed, softmax_scale):
    scores = exact_einsum('crgd,ckgd->crgk', queries, keys_part) * softmax_scale
    weights = jnp.exp(scores - row_max[..., None])
    probability = weights / row_total[..., None]
    d_widened = d_mixed.astype(jnp.float32)
    scaled_grad = (d_widened / row_total[..., None]).astype(jnp.bfloat16)
    d_values = exact_einsum('crgk,crgd->ckgd', weights.astype(jnp.bfloat16), scaled_grad)
    d_probs = exact_einsum('crgd,ckgd->crgk', d_mixed, values_part)
    row_delta = lax.optimization_barrier(jnp.sum(d_widened * attended, axis=-1))
    d_scores = (probability * (d_probs - row_delta[..., None])).astype(jnp.bfloat16)
    d_queries = exact_einsum('crgk,ckgd->crgd', d_scores, keys_part) * softmax_scale + d_widened
    d_keys = exact_einsum('crgk,crgd->ckgd', d_scores, queries) * softmax_scale
    return (d_queries, d_keys, d_values)

def reference(tokens, qkv_weight, pool_kernel, norm_gain, out_weight, out_cotangent):
    model_width = tokens.shape[-1]
    head_size = model_width // HEADS
    softmax_scale = head_size ** (-0.5)
    kernel_taps = tap_table(pool_kernel, HEADS)

    def one_clip(members):
        clip_tokens, clip_cotangent = members
        token_rows = clip_tokens.reshape(-1, model_width)
        projected = jnp.dot(token_rows, qkv_weight, preferred_element_type=jnp.float32).astype(jnp.bfloat16)
        queries = projected[:, :model_width].reshape(1, -1, HEADS, head_size)
        volume = projected[:, model_width:].reshape(1, FRAMES, GRID_H, GRID_W, 2 * model_width)
        own_blocks = cut_blocks(volume)
        partials = spatial_sums(own_blocks, kernel_taps)
        zeros_frame = jnp.zeros_like(partials[0][:, :1])
        pooled_sum = jnp.concatenate([zeros_frame, partials[0][:, :-1]], axis=1) + partials[1] + jnp.concatenate([partials[2][:, 1:], zeros_frame], axis=1)
        pooled, normed, inv_std = pooled_norm(pooled_sum, norm_gain, HEADS)
        pooled = pooled.reshape(1, -1, 2 * model_width)
        keys_all = pooled[..., :model_width].reshape(1, -1, HEADS, head_size)
        values_all = pooled[..., model_width:].reshape(1, -1, HEADS, head_size)
        row_max, row_total, weighted = by_pairs(partial(group_forward, softmax_scale=softmax_scale), (queries, keys_all, values_all))
        attended = weighted / row_total[..., None]
        mixed = (attended + queries.astype(jnp.float32)).astype(jnp.bfloat16)
        mixed_rows = mixed.reshape(-1, model_width)
        block_out = jnp.dot(mixed_rows, out_weight, preferred_element_type=jnp.float32).astype(jnp.bfloat16)
        cotangent_rows = clip_cotangent.reshape(-1, model_width)
        d_mixed = jnp.dot(cotangent_rows, out_weight.T, preferred_element_type=jnp.float32).astype(jnp.bfloat16)
        d_mixed = d_mixed.reshape(1, -1, HEADS, head_size)
        out_local = jnp.dot(mixed_rows.T, cotangent_rows, preferred_element_type=jnp.float32)
        d_queries, d_keys, d_values = by_pairs(partial(group_backward, softmax_scale=softmax_scale), (queries, keys_all, values_all, row_max, row_total, attended, d_mixed))
        d_pooled = jnp.concatenate([d_keys.reshape(1, -1, model_width), d_values.reshape(1, -1, model_width)], axis=-1)
        d_grouped = d_pooled.reshape(normed.shape)
        sum_axes = tuple(range(normed.ndim - 3)) + (normed.ndim - 2,)
        gain_local = lax.optimization_barrier(jnp.sum(d_grouped * normed, axis=sum_axes))
        d_normed = d_grouped * norm_gain[:, None, :]
        d_summed = inv_std * (d_normed - lax.optimization_barrier(jnp.mean(d_normed, axis=-1, keepdims=True)) - normed * lax.optimization_barrier(jnp.mean(d_normed * normed, axis=-1, keepdims=True)))
        d_summed = d_summed.reshape(pooled_sum.shape)
        rims = jnp.pad(d_summed, ((0, 0), (1, 1), (0, 0), (0, 0), (0, 0)))
        shifted = [rims[:, 2:], rims[:, 1:FRAMES + 1], rims[:, :FRAMES]]
        d_volume = spread_taps(shifted, kernel_taps, GRID_H, GRID_W)
        kernel_local = tap_grads(shifted, own_blocks, HEADS)
        d_projected = jnp.concatenate([d_queries.reshape(-1, model_width), d_volume.reshape(-1, 2 * model_width)], axis=-1).astype(jnp.bfloat16)
        grad_rows = jnp.dot(d_projected, qkv_weight.T, preferred_element_type=jnp.float32).astype(jnp.bfloat16)
        qkv_local = jnp.dot(token_rows.T, d_projected, preferred_element_type=jnp.float32)
        return (block_out.reshape(clip_tokens.shape), grad_rows.reshape(clip_tokens.shape), qkv_local, out_local, kernel_local, gain_local)
    results = lax.map(one_clip, (tokens, out_cotangent))
    norm_scale = float(TOKENS) ** (-0.5)
    return (results[0], results[1], lax.optimization_barrier(jnp.sum(results[2], axis=0)) * norm_scale, lax.optimization_barrier(jnp.sum(results[3], axis=0)) * norm_scale, lax.optimization_barrier(jnp.sum(results[4], axis=0)) * norm_scale, lax.optimization_barrier(jnp.sum(results[5], axis=0)) * norm_scale)
```

```python
import functools

import jax
import jax.numpy as jnp
import numpy as np
from jax import lax
from jax.experimental import pallas as pl
from jax.experimental.pallas import tpu as pltpu
from jax.sharding import PartitionSpec as P

HEADS = 12
GRID_H = 32
EPSILON = 1e-05
STRIDE = 4
LANES = 128
f32 = jnp.float32
bf16 = jnp.bfloat16
MESH = pl.DeviceIdType.MESH


def mm(a, b, ca=1, cb=0, precision=None):
    return lax.dot_general(
        a, b, (((ca,), (cb,)), ((), ())), preferred_element_type=f32, precision=precision
    )


def selection(cells, breadth):
    height = cells // breadth
    ph, pw = height // STRIDE, breadth // STRIDE
    sel = np.zeros((3, 3, ph, pw, height, breadth), np.float32)
    for b in range(3):
        for e in range(3):
            for i in range(ph):
                for u in range(pw):
                    y, x = STRIDE * i + b - 1, STRIDE * u + e - 1
                    if 0 <= y < height and 0 <= x < breadth:
                        sel[b, e, i, u, y, x] = 1.0
    return sel.reshape(9 * ph * pw, cells)


def stage_list(dp_size, tm_size):
    stages = []
    bit = 1
    while bit < dp_size:
        stages.append(("dp", bit))
        bit *= 2
    if tm_size > 1:
        stages.append(("tm", 1))
    bit = tm_size // 2
    while bit > 1:
        stages.append(("tm", bit))
        bit //= 2
    return stages


def block_index(stages, dp, tm):
    index = 0
    for axis, bit in stages:
        index = index * 2 + ((dp if axis == "dp" else tm) // bit) % 2
    return index


def kernel(
    dp_size, tm_size, stages, norm_scale,
    tok, wqkv, taps, wout, cot, sel,
    block_out, grad_tok, grad_qkv, grad_out, small_out,
    proj, blocks, dmix, mixed, dproj, gath, dpart, drecv,
    part_lo, part_mid, part_hi, in_lo, in_hi, normed, inv, dsum, in_next, in_prev,
    contrib, tok_t, acc, send, recv, fin, kacc, sbuf, srecv,
    halo_send, halo_recv, ag_send, ag_recv, rs_send, rs_recv,
    gr_send, gr_recv, sm_send, sm_recv, fin_send, fin_recv,
):
    cells, width = tok.shape
    wide = 2 * width
    pooled = sel.shape[0] // 9
    keys = tm_size * pooled
    scale = (width // HEADS) ** (-0.5)
    chunks = wide // LANES
    half_chunks = width // LANES
    rows = width // tm_size
    group = wide // dp_size
    blocks_all = dp_size * tm_size
    me_d = lax.axis_index("dp")
    me_t = lax.axis_index("tm")
    tile = 2 * LANES

    barrier = pltpu.get_barrier_semaphore()
    for k in range(1, tm_size):
        pl.semaphore_signal(
            barrier, inc=1, device_id={"tm": (me_t + k) % tm_size}, device_id_type=MESH
        )
    for k in range(1, dp_size):
        pl.semaphore_signal(
            barrier, inc=1, device_id={"dp": (me_d + k) % dp_size}, device_id_type=MESH
        )

    has_next = me_t < tm_size - 1
    has_prev = me_t > 0

    def remote(src, dst, ssem, rsem, where):
        return pltpu.make_async_remote_copy(
            src_ref=src, dst_ref=dst, send_sem=ssem, recv_sem=rsem,
            device_id=where, device_id_type=MESH,
        )

    def halo_up(src, dst, slot):
        return remote(src, dst, halo_send.at[slot], halo_recv.at[slot],
                      {"tm": (me_t + 1) % tm_size})

    def halo_down(src, dst, slot):
        return remote(src, dst, halo_send.at[slot], halo_recv.at[slot],
                      {"tm": (me_t + tm_size - 1) % tm_size})

    def halo_start(up_src, up_dst, down_src, down_dst, slot):
        @pl.when(has_next)
        def _():
            halo_up(up_src, up_dst, slot).start()

        @pl.when(has_prev)
        def _():
            halo_down(down_src, down_dst, slot + 1).start()

    def halo_wait(up_src, up_dst, down_src, down_dst, slot):
        @pl.when(has_next)
        def _():
            halo_up(up_src, up_dst, slot).wait_send()
            halo_down(down_src, down_dst, slot + 1).wait_recv()

        @pl.when(has_prev)
        def _():
            halo_down(down_src, down_dst, slot + 1).wait_send()
            halo_up(up_src, up_dst, slot).wait_recv()

    def cols(c, size=LANES, base=0):
        return pl.ds(pl.multiple_of(base + c * size, LANES), size)

    @pl.loop(0, wide // tile)
    def _(c):
        value = mm(tok[...], wqkv[:, cols(c, tile, width)]).astype(bf16)
        blocks[:, cols(c, tile)] = mm(sel[...], value).astype(bf16)

    @pl.loop(0, chunks)
    def _(c):
        s = c // half_chunks
        sums = [None, None, None]
        for p in range(9):
            value = blocks[p * pooled:(p + 1) * pooled, cols(c)].astype(f32)
            for t in range(3):
                term = value * taps[s, pl.ds(t * 9 + p, 1), :]
                sums[t] = term if sums[t] is None else sums[t] + term
        part_lo[:, cols(c)] = sums[0]
        part_mid[:, cols(c)] = sums[1]
        part_hi[:, cols(c)] = sums[2]

    pl.semaphore_wait(barrier, tm_size - 1 + dp_size - 1)
    first = (part_lo, in_lo, part_hi, in_hi, 0)
    halo_start(*first)

    @pl.when(jnp.logical_not(has_prev))
    def _():
        in_lo[...] = jnp.zeros_like(in_lo)

    @pl.when(jnp.logical_not(has_next))
    def _():
        in_hi[...] = jnp.zeros_like(in_hi)

    @pl.loop(0, width // tile)
    def _(c):
        proj[:, cols(c, tile)] = mm(tok[...], wqkv[:, cols(c, tile)]).astype(bf16)

    row = lax.broadcasted_iota(jnp.int32, (LANES, LANES), 0)
    col = lax.broadcasted_iota(jnp.int32, (LANES, LANES), 1)
    head = width // HEADS
    same = jnp.where((row < head) == (col < head), 1.0, 0.0).astype(f32)

    def group_mean(x):
        return mm(x, same, precision=lax.Precision.HIGHEST) * (1.0 / head)

    halo_wait(*first)

    @pl.loop(0, chunks)
    def _(c):
        s = c // half_chunks
        total = in_lo[:, cols(c)] + part_mid[:, cols(c)] + in_hi[:, cols(c)]
        centred = total - group_mean(total)
        inv_std = lax.rsqrt(group_mean(centred * centred) + EPSILON)
        norm = centred * inv_std
        normed[:, cols(c)] = norm
        inv[:, cols(c)] = inv_std
        gath[me_t, :, cols(c)] = (norm * taps[s, pl.ds(27, 1), :]).astype(bf16)

    def gather_copy(k):
        return remote(gath.at[me_t], gath.at[me_t], ag_send.at[k - 1], ag_recv.at[k - 1],
                      {"tm": (me_t + k) % tm_size})

    def gather_arrival(k):
        source = (me_t + tm_size - k) % tm_size
        return remote(gath.at[source], gath.at[source], ag_send.at[k - 1], ag_recv.at[k - 1],
                      {"tm": (me_t + k) % tm_size})

    for k in range(1, tm_size):
        gather_copy(k).start()

    @pl.loop(0, width // tile)
    def _(c):
        dmix[:, cols(c, tile)] = mm(
            cot[...], wout[pl.ds(pl.multiple_of(c * tile, tile), tile), :], 1, 1
        ).astype(bf16)

    @pl.loop(0, width // LANES)
    def _(c):
        tok_t[pl.ds(pl.multiple_of(c * LANES, LANES), LANES), :] = tok[:, cols(c)].T

    for k in range(1, tm_size):
        gather_copy(k).wait_send()
        gather_arrival(k).wait_recv()

    lane = lax.broadcasted_iota(jnp.int32, (1, LANES), 1)

    @pl.loop(0, half_chunks)
    def _(c):
        q = proj[:, cols(c)]
        k = gath[:, :, cols(c)].reshape(keys, LANES)
        v = gath[:, :, cols(c, LANES, width)].reshape(keys, LANES)
        dm = dmix[:, cols(c)]
        mixed_sum = q.astype(f32)
        dq_sum = dk_sum = dv_sum = None
        for a in range(2):
            mask = jnp.where((lane < head) == (a == 0), 1.0, 0.0).astype(f32)
            mask_b = mask.astype(bf16)
            k_a = k * mask_b
            scores = mm(q, k_a, 1, 1) * scale
            weights = jnp.exp(scores - jnp.max(scores, axis=-1, keepdims=True))
            inv_total = 1.0 / jnp.sum(weights, axis=-1, keepdims=True)
            rounded = weights.astype(bf16)
            attended = mm(rounded, v) * inv_total * mask
            mixed_sum = mixed_sum + attended
            dm_a = dm * mask_b
            dm_f = dm_a.astype(f32)
            scaled_grad = (dm_f * inv_total).astype(bf16)
            dv = mm(rounded, scaled_grad, 0, 0)
            d_probs = mm(dm_a, v, 1, 1)
            delta = jnp.sum(dm_f * attended, axis=-1, keepdims=True)
            ds = (weights * inv_total * (d_probs - delta)).astype(bf16)
            dq = mm(ds, k_a)
            dk = mm(ds, q * mask_b, 0, 0)
            dq_sum = dq if a == 0 else dq_sum + dq
            dk_sum = dk if a == 0 else dk_sum + dk
            dv_sum = dv if a == 0 else dv_sum + dv
        mixed[:, cols(c)] = mixed_sum.astype(bf16)
        dproj[:, cols(c)] = (dq_sum * scale + dm.astype(f32)).astype(bf16)
        dpart[:, :, cols(c)] = (dk_sum * scale).astype(bf16).reshape(tm_size, pooled, LANES)
        dpart[:, :, cols(c, LANES, width)] = dv_sum.astype(bf16).reshape(tm_size, pooled, LANES)

    def scatter_copy(k):
        target = (me_t + k) % tm_size
        return remote(dpart.at[target], drecv.at[k - 1], rs_send.at[k - 1], rs_recv.at[k - 1],
                      {"tm": target})

    for k in range(1, tm_size):
        scatter_copy(k).start()

    starts = []
    at = 0
    for s in range(len(stages)):
        starts.append(at)
        at += blocks_all >> (s + 1)

    def my_bit(s):
        axis, bit = stages[s]
        return ((me_d if axis == "dp" else me_t) // bit) % 2

    def peer(s):
        axis, bit = stages[s]
        me = me_d if axis == "dp" else me_t
        return {axis: me + bit * (1 - 2 * my_bit(s))}

    def base(s):
        at = 0
        for i in range(s):
            at = at + my_bit(i) * (blocks_all >> (i + 1))
        return at

    def halving_copy(part, s):
        span = pl.ds(starts[s], blocks_all >> (s + 1))
        return remote(send.at[part, span], recv.at[part, span], gr_send.at[part, s],
                      gr_recv.at[part, s], peer(s))

    def halving_start(part, s):
        count = blocks_all >> (s + 1)
        other = base(s) + (1 - my_bit(s)) * count

        @pl.loop(0, count)
        def _(i):
            send[part, starts[s] + i] = acc[part, other + i].astype(bf16)

        halving_copy(part, s).start()

    def halving_wait(part, s):
        count = blocks_all >> (s + 1)
        mine = base(s) + my_bit(s) * count
        halving_copy(part, s).wait()

        @pl.loop(0, count)
        def _(i):
            acc[part, mine + i] = acc[part, mine + i] + recv[part, starts[s] + i].astype(f32)

    def put(part, column, value):
        size = value.shape[1]
        value = value.reshape(tm_size, rows, size)
        for w in range(0, size, LANES):
            g, inside = divmod(column + w, group)
            for j in range(tm_size):
                acc[part, block_index(stages, g, j), :, inside:inside + LANES] = (
                    value[j, :, w:w + LANES]
                )

    def fin_copy(part, k):
        return remote(fin.at[part, 0], fin.at[part, k], fin_send.at[part, k - 1],
                      fin_recv.at[part, k - 1], {"dp": (me_d + k) % dp_size})

    def fin_start(part):
        fin[part, 0] = (acc[part, base(len(stages))] * norm_scale).astype(bf16)
        for k in range(1, dp_size):
            fin_copy(part, k).start()

    def fin_wait(part):
        for k in range(1, dp_size):
            fin_copy(part, k).wait()

    for c in range(width // tile):
        put(0, c * tile, mm(mixed[...], cot[:, c * tile:(c + 1) * tile], 0, 0))
    for c in range(width // tile):
        put(0, width + c * tile, mm(tok_t[...], dproj[:, c * tile:(c + 1) * tile]))
    halving_start(0, 0)

    @pl.loop(0, width // tile)
    def _(c):
        block_out[:, cols(c, tile)] = mm(mixed[...], wout[:, cols(c, tile)]).astype(bf16)

    halving_wait(0, 0)
    halving_start(0, 1)

    for k in range(1, tm_size):
        scatter_copy(k).wait()

    kacc[...] = jnp.zeros_like(kacc)

    def fold(x):
        return jnp.sum(x.reshape(pooled // 8, 8, LANES), axis=0)

    @pl.loop(0, chunks)
    def _(c):
        s = c // half_chunks
        total = dpart[me_t, :, cols(c)].astype(f32)
        for k in range(1, tm_size):
            total = total + drecv[k - 1, :, cols(c)].astype(f32)
        norm = normed[:, cols(c)]
        kacc[s, 27] += fold(total * norm)
        dn = total * taps[s, pl.ds(27, 1), :]
        dsum[:, cols(c)] = inv[:, cols(c)] * (
            dn - group_mean(dn) - norm * group_mean(dn * norm)
        )

    second = (dsum, in_prev, dsum, in_next, 2)
    halo_start(*second)

    @pl.when(jnp.logical_not(has_prev))
    def _():
        in_prev[...] = jnp.zeros_like(in_prev)

    @pl.when(jnp.logical_not(has_next))
    def _():
        in_next[...] = jnp.zeros_like(in_next)

    halving_wait(0, 1)
    halo_wait(*second)
    halving_start(0, 2)

    @pl.loop(0, chunks)
    def _(c):
        s = c // half_chunks
        shifted = (in_next[:, cols(c)], dsum[:, cols(c)], in_prev[:, cols(c)])
        for p in range(9):
            value = blocks[p * pooled:(p + 1) * pooled, cols(c)].astype(f32)
            spread = None
            for t in range(3):
                kacc[s, t * 9 + p] += fold(shifted[t] * value)
                term = shifted[t] * taps[s, pl.ds(t * 9 + p, 1), :]
                spread = term if spread is None else spread + term
            contrib[p * pooled:(p + 1) * pooled, cols(c)] = spread.astype(bf16)

    sbuf[0] = jnp.sum(kacc[...], axis=2)

    for c in range(wide // tile):
        dv = mm(sel[...], contrib[:, c * tile:(c + 1) * tile], 0, 0).astype(bf16)
        dproj[:, width + c * tile:width + (c + 1) * tile] = dv
        put(1, c * tile, mm(tok_t[...], dv))

    def small_copy(s):
        return remote(sbuf.at[s], srecv.at[s], sm_send.at[s], sm_recv.at[s], peer(s))

    def small_wait(s):
        small_copy(s).wait()
        sbuf[s + 1] = sbuf[s] + srecv[s]

    count = len(stages)
    halving_start(1, 0)
    small_copy(0).start()

    @pl.loop(0, width // tile)
    def _(c):
        at = pl.ds(pl.multiple_of(c * tile, tile), tile)
        grad_tok[:, cols(c, tile)] = mm(dproj[...], wqkv[at, :], 1, 1).astype(bf16)

    halving_wait(1, 0)
    small_wait(0)
    later = 3
    done = False
    for s in range(1, count):
        halving_start(1, s)
        small_copy(s).start()
        if later <= count:
            halving_wait(0, later - 1)
            if later < count:
                halving_start(0, later)
            later += 1
        elif not done:
            fin_start(0)
            done = True
        halving_wait(1, s)
        small_wait(s)
    while later <= count:
        halving_wait(0, later - 1)
        if later < count:
            halving_start(0, later)
        later += 1
    if not done:
        fin_start(0)
    fin_start(1)
    small_out[...] = sbuf[count] * norm_scale
    fin_wait(0)
    fin_wait(1)
    for part in range(2):
        for k in range(dp_size):
            g = (me_d + dp_size - k) % dp_size
            for w in range(0, group, LANES):
                value = fin[part, k, :, w:w + LANES].astype(f32)
                if part == 1:
                    grad_qkv[:, cols(0, LANES, width + g * group + w)] = value
                else:
                    column = g * group + w

                    @pl.when(column < width)
                    def _(value=value, column=column):
                        grad_out[:, cols(0, LANES, column % width)] = value

                    @pl.when(column >= width)
                    def _(value=value, column=column):
                        grad_qkv[:, cols(0, LANES, column % width)] = value


def shards(dp_size, tm_size, tokens, qkv_weight, pool_kernel, norm_gain, out_weight, cotangent):
    cells, width = tokens.shape[2:]
    wide = 2 * width
    stages = stage_list(dp_size, tm_size)
    blocks_all = dp_size * tm_size
    sel = jnp.asarray(selection(cells, cells // GRID_H), bf16)
    pooled = sel.shape[0] // 9
    rows = width // tm_size
    group = wide // dp_size
    norm_scale = float(blocks_all * cells) ** (-0.5)
    taps = jnp.concatenate([pool_kernel, norm_gain[:, None, :]], axis=1)
    taps = jnp.concatenate([taps, taps], axis=-1)
    taps_rows = taps.shape[1]
    vmem = pl.BlockSpec(memory_space=pltpu.VMEM)
    count = len(stages)
    dma = pltpu.SemaphoreType.DMA
    small = (pooled, wide)
    block_out, grad_tok, grad_qkv, grad_out, total = pl.pallas_call(
        functools.partial(kernel, dp_size, tm_size, stages, norm_scale),
        out_shape=[
            jax.ShapeDtypeStruct((cells, width), bf16),
            jax.ShapeDtypeStruct((cells, width), bf16),
            jax.ShapeDtypeStruct((rows, 3 * width), f32),
            jax.ShapeDtypeStruct((rows, width), f32),
            jax.ShapeDtypeStruct((2, taps_rows, LANES), f32),
        ],
        in_specs=[vmem] * 6,
        out_specs=[vmem] * 5,
        scratch_shapes=[
            pltpu.VMEM((cells, width), bf16),
            pltpu.VMEM((9 * pooled, wide), bf16),
            pltpu.VMEM((cells, width), bf16),
            pltpu.VMEM((cells, width), bf16),
            pltpu.VMEM((cells, 3 * width), bf16),
            pltpu.VMEM((tm_size, pooled, wide), bf16),
            pltpu.VMEM((tm_size, pooled, wide), bf16),
            pltpu.VMEM((tm_size - 1, pooled, wide), bf16),
        ]
        + [pltpu.VMEM(small, f32)] * 10
        + [
            pltpu.VMEM((9 * pooled, wide), bf16),
            pltpu.VMEM((width, cells), bf16),
            pltpu.VMEM((2, blocks_all, rows, group), f32),
            pltpu.VMEM((2, blocks_all, rows, group), bf16),
            pltpu.VMEM((2, blocks_all, rows, group), bf16),
            pltpu.VMEM((2, dp_size, rows, group), bf16),
            pltpu.VMEM((2, taps_rows, 8, LANES), f32),
            pltpu.VMEM((count + 1, 2, taps_rows, LANES), f32),
            pltpu.VMEM((count, 2, taps_rows, LANES), f32),
            dma((4,)),
            dma((4,)),
            dma((tm_size - 1,)),
            dma((tm_size - 1,)),
            dma((tm_size - 1,)),
            dma((tm_size - 1,)),
            dma((2, count)),
            dma((2, count)),
            dma((count,)),
            dma((count,)),
            dma((2, dp_size - 1)),
            dma((2, dp_size - 1)),
        ],
        compiler_params=pltpu.CompilerParams(
            collective_id=0, has_side_effects=True, vmem_limit_bytes=63 * 1024 * 1024
        ),
        cost_estimate=pl.CostEstimate(
            flops=10 * 10**9, bytes_accessed=10 * 10**6, transcendentals=0
        ),
    )(
        tokens.reshape(cells, width), qkv_weight, taps, out_weight,
        cotangent.reshape(cells, width), sel,
    )
    head = width // HEADS
    summed = total[:, :, :head] + total[:, :, head:]
    return (
        block_out.reshape(tokens.shape), grad_tok.reshape(tokens.shape), grad_qkv, grad_out,
        summed[:, :-1], summed[:, -1],
    )


def solution(mesh):
    placed = (P("dp", "tm", None, None), P(), P(), P(), P(), P("dp", "tm", None, None))
    return jax.shard_map(
        functools.partial(shards, mesh.shape["dp"], mesh.shape["tm"]),
        mesh=mesh,
        in_specs=placed,
        out_specs=(
            P("dp", "tm", None, None),
            P("dp", "tm", None, None),
            P("tm", None),
            P("tm", None),
            P(),
            P(),
        ),
        check_vma=False,
    )
```

```python
import functools

import jax
import jax.numpy as jnp
import numpy as np
from jax import lax
from jax.experimental import pallas as pl
from jax.experimental.pallas import tpu as pltpu
from jax.sharding import PartitionSpec as P

HEADS = 12
GRID_H = 32
EPSILON = 1e-05
STRIDE = 4
LANES = 128
f32 = jnp.float32
bf16 = jnp.bfloat16
MESH = pl.DeviceIdType.MESH


def mm(a, b, ca=1, cb=0, precision=None):
    return lax.dot_general(
        a, b, (((ca,), (cb,)), ((), ())), preferred_element_type=f32, precision=precision
    )


def selection(cells, breadth):
    height = cells // breadth
    ph, pw = height // STRIDE, breadth // STRIDE
    sel = np.zeros((3, 3, ph, pw, height, breadth), np.float32)
    for b in range(3):
        for e in range(3):
            for i in range(ph):
                for u in range(pw):
                    y, x = STRIDE * i + b - 1, STRIDE * u + e - 1
                    if 0 <= y < height and 0 <= x < breadth:
                        sel[b, e, i, u, y, x] = 1.0
    return sel.reshape(9 * ph * pw, cells)


def stage_list(dp_size, tm_size, dp_first):
    over_dp, over_tm = [], []
    bit = 1
    while bit < dp_size:
        over_dp.append(("dp", bit))
        bit *= 2
    if tm_size > 1:
        over_tm.append(("tm", 1))
    bit = tm_size // 2
    while bit > 1:
        over_tm.append(("tm", bit))
        bit //= 2
    if dp_first:
        return over_dp + over_tm
    return over_dp[:1] + over_tm + over_dp[1:]


def block_index(stages, dp, tm):
    index = 0
    for axis, bit in stages:
        index = index * 2 + ((dp if axis == "dp" else tm) // bit) % 2
    return index


def kernel(
    dp_size, tm_size, orders, norm_scale,
    tok, wqkv, taps, wout, cot, sel,
    block_out, grad_tok, grad_qkv, grad_out, small_out,
    proj, blocks, dmix, mixed, dproj, gath, dpart, drecv,
    zsend, zrecv, part_lo, part_mid, part_hi, in_lo, in_hi, normed, inv, dsum,
    dsum_b, in_next, in_prev, contrib, tok_t,
    acc_a, acc_b, acc_c, send_a, send_b, send_c, recv_a, recv_b, recv_c, fin_a, fin_b, fin_c,
    kacc, sbuf, srecv,
    halo_send, halo_recv, ag_send, ag_recv, rs_send, rs_recv, rz_send, rz_recv,
    gr_send, gr_recv, sm_send, sm_recv, fin_send, fin_recv,
):
    cells, width = tok.shape
    wide = 2 * width
    pooled = sel.shape[0] // 9
    keys = tm_size * pooled
    scale = (width // HEADS) ** (-0.5)
    chunks = wide // LANES
    half_chunks = width // LANES
    rows = width // tm_size
    group = wide // dp_size
    blocks_all = dp_size * tm_size
    me_d = lax.axis_index("dp")
    me_t = lax.axis_index("tm")
    tile = 2 * LANES
    column = tm_size // 2
    pair = me_t + 1 - 2 * (me_t % 2)
    third = half_chunks // 2
    accs, sends, recvs = (acc_a, acc_b, acc_c), (send_a, send_b, send_c), (recv_a, recv_b, recv_c)
    fins = (fin_a, fin_b, fin_c)

    barrier = pltpu.get_barrier_semaphore()
    for k in range(1, tm_size):
        pl.semaphore_signal(
            barrier, inc=1, device_id={"tm": (me_t + k) % tm_size}, device_id_type=MESH
        )
    for k in range(1, dp_size):
        pl.semaphore_signal(
            barrier, inc=1, device_id={"dp": (me_d + k) % dp_size}, device_id_type=MESH
        )

    has_next = me_t < tm_size - 1
    has_prev = me_t > 0

    def remote(src, dst, ssem, rsem, where):
        return pltpu.make_async_remote_copy(
            src_ref=src, dst_ref=dst, send_sem=ssem, recv_sem=rsem,
            device_id=where, device_id_type=MESH,
        )

    def halo_up(src, dst, slot):
        return remote(src, dst, halo_send.at[slot], halo_recv.at[slot],
                      {"tm": (me_t + 1) % tm_size})

    def halo_down(src, dst, slot):
        return remote(src, dst, halo_send.at[slot], halo_recv.at[slot],
                      {"tm": (me_t + tm_size - 1) % tm_size})

    def halo_start(up_src, up_dst, down_src, down_dst, slot):
        @pl.when(has_next)
        def _():
            halo_up(up_src, up_dst, slot).start()

        @pl.when(has_prev)
        def _():
            halo_down(down_src, down_dst, slot + 1).start()

    def halo_wait(up_src, up_dst, down_src, down_dst, slot):
        @pl.when(has_next)
        def _():
            halo_up(up_src, up_dst, slot).wait_send()
            halo_down(down_src, down_dst, slot + 1).wait_recv()

        @pl.when(has_prev)
        def _():
            halo_down(down_src, down_dst, slot + 1).wait_send()
            halo_up(up_src, up_dst, slot).wait_recv()

    def cols(c, size=LANES, base=0):
        return pl.ds(pl.multiple_of(base + c * size, LANES), size)

    def first(s):
        at = pl.ds(s * width, width)
        return (part_lo.at[:, at], in_lo.at[:, at], part_hi.at[:, at], in_hi.at[:, at], 2 * s)

    for s in range(2):
        @pl.loop(0, width // tile)
        def _(c, s=s):
            value = mm(tok[...], wqkv[:, cols(c, tile, width + s * width)]).astype(bf16)
            blocks[:, cols(c, tile, s * width)] = mm(sel[...], value).astype(bf16)

        @pl.loop(0, half_chunks)
        def _(c, s=s):
            here = cols(c, LANES, s * width)
            sums = [None, None, None]
            for p in range(9):
                value = blocks[p * pooled:(p + 1) * pooled, here].astype(f32)
                for t in range(3):
                    term = value * taps[s, pl.ds(t * 9 + p, 1), :]
                    sums[t] = term if sums[t] is None else sums[t] + term
            part_lo[:, here] = sums[0]
            part_mid[:, here] = sums[1]
            part_hi[:, here] = sums[2]

        if s == 0:
            pl.semaphore_wait(barrier, tm_size - 1 + dp_size - 1)
        halo_start(*first(s))

    @pl.when(jnp.logical_not(has_prev))
    def _():
        in_lo[...] = jnp.zeros_like(in_lo)

    @pl.when(jnp.logical_not(has_next))
    def _():
        in_hi[...] = jnp.zeros_like(in_hi)

    @pl.loop(0, width // tile)
    def _(c):
        proj[:, cols(c, tile)] = mm(tok[...], wqkv[:, cols(c, tile)]).astype(bf16)

    row = lax.broadcasted_iota(jnp.int32, (LANES, LANES), 0)
    col = lax.broadcasted_iota(jnp.int32, (LANES, LANES), 1)
    head = width // HEADS
    same = jnp.where((row < head) == (col < head), 1.0, 0.0).astype(f32)

    def group_mean(x):
        return mm(x, same, precision=lax.Precision.HIGHEST) * (1.0 / head)

    for s in range(2):
        halo_wait(*first(s))

    @pl.loop(0, chunks)
    def _(c):
        s = c // half_chunks
        total = in_lo[:, cols(c)] + part_mid[:, cols(c)] + in_hi[:, cols(c)]
        centred = total - group_mean(total)
        inv_std = lax.rsqrt(group_mean(centred * centred) + EPSILON)
        norm = centred * inv_std
        normed[:, cols(c)] = norm
        inv[:, cols(c)] = inv_std
        gath[me_t, :, cols(c)] = (norm * taps[s, pl.ds(27, 1), :]).astype(bf16)

    def column_slot(k, back):
        return (back + tm_size - 2 * k) % tm_size

    def along(k, slot):
        return remote(gath.at[slot], gath.at[slot], ag_send.at[0, k], ag_recv.at[0, k],
                      {"tm": (me_t + 2 * k) % tm_size})

    def across(k, slot):
        return remote(gath.at[slot], gath.at[slot], ag_send.at[1, k], ag_recv.at[1, k],
                      {"tm": pair})

    for k in range(1, column):
        along(k, me_t).start()
    across(0, me_t).start()

    @pl.loop(0, width // tile)
    def _(c):
        dmix[:, cols(c, tile)] = mm(
            cot[...], wout[pl.ds(pl.multiple_of(c * tile, tile), tile), :], 1, 1
        ).astype(bf16)

    for k in range(1, column):
        along(k, column_slot(k, me_t)).wait_recv()
        across(k, column_slot(k, me_t)).start()

    @pl.loop(0, width // LANES)
    def _(c):
        tok_t[pl.ds(pl.multiple_of(c * LANES, LANES), LANES), :] = tok[:, cols(c)].T

    for k in range(1, column):
        along(k, me_t).wait_send()
    for k in range(column):
        across(k, column_slot(k, pair)).wait_recv()
        across(k, column_slot(k, me_t)).wait_send()

    lane = lax.broadcasted_iota(jnp.int32, (1, LANES), 1)

    def attention(h, i):
        c = h * third + i
        q = proj[:, cols(c)]
        k = gath[:, :, cols(c)].reshape(keys, LANES)
        v = gath[:, :, cols(c, LANES, width)].reshape(keys, LANES)
        dm = dmix[:, cols(c)]
        mixed_sum = q.astype(f32)
        dq_sum = dk_sum = dv_sum = None
        for a in range(2):
            mask = jnp.where((lane < head) == (a == 0), 1.0, 0.0).astype(f32)
            mask_b = mask.astype(bf16)
            k_a = k * mask_b
            scores = mm(q, k_a, 1, 1) * scale
            weights = jnp.exp(scores - jnp.max(scores, axis=-1, keepdims=True))
            inv_total = 1.0 / jnp.sum(weights, axis=-1, keepdims=True)
            rounded = weights.astype(bf16)
            attended = mm(rounded, v) * inv_total * mask
            mixed_sum = mixed_sum + attended
            dm_a = dm * mask_b
            dm_f = dm_a.astype(f32)
            scaled_grad = (dm_f * inv_total).astype(bf16)
            dv = mm(rounded, scaled_grad, 0, 0)
            d_probs = mm(dm_a, v, 1, 1)
            delta = jnp.sum(dm_f * attended, axis=-1, keepdims=True)
            ds = (weights * inv_total * (d_probs - delta)).astype(bf16)
            dq = mm(ds, k_a)
            dk = mm(ds, q * mask_b, 0, 0)
            dq_sum = dq if a == 0 else dq_sum + dq
            dk_sum = dk if a == 0 else dk_sum + dk
            dv_sum = dv if a == 0 else dv_sum + dv
        mixed[:, cols(c)] = mixed_sum.astype(bf16)
        dproj[:, cols(c)] = (dq_sum * scale + dm.astype(f32)).astype(bf16)
        shape = (tm_size, pooled, LANES)
        dpart[h, :, :, cols(i)] = (dk_sum * scale).astype(bf16).reshape(shape)
        dpart[h, :, :, cols(third + i)] = dv_sum.astype(bf16).reshape(shape)

    def reduce_across(h, k):
        return remote(dpart.at[h, (pair + 2 * k) % tm_size], drecv.at[h, k], rs_send.at[h, k],
                      rs_recv.at[h, k], {"tm": pair})

    def reduce_along(h, k):
        return remote(zsend.at[h, k - 1], zrecv.at[h, k - 1], rz_send.at[h, k - 1],
                      rz_recv.at[h, k - 1], {"tm": (me_t + 2 * k) % tm_size})

    def pass_on(h):
        for k in range(1, column):
            reduce_across(h, k).wait()
            mine = dpart[h, (me_t + 2 * k) % tm_size].astype(f32)
            zsend[h, k - 1] = (mine + drecv[h, k].astype(f32)).astype(bf16)
            reduce_along(h, k).start()
        reduce_across(h, 0).wait()

    for h in range(2):
        @pl.loop(0, third)
        def _(i, h=h):
            attention(h, i)

        for k in list(range(1, column)) + [0]:
            reduce_across(h, k).start()

    count = len(orders[0])
    starts = []
    at = 0
    for s in range(count):
        starts.append(at)
        at += blocks_all >> (s + 1)

    def my_bit(part, s):
        axis, bit = orders[part][s]
        return ((me_d if axis == "dp" else me_t) // bit) % 2

    def peer(part, s):
        axis, bit = orders[part][s]
        me = me_d if axis == "dp" else me_t
        return {axis: me + bit * (1 - 2 * my_bit(part, s))}

    def base(part, s):
        at = 0
        for i in range(s):
            at = at + my_bit(part, i) * (blocks_all >> (i + 1))
        return at

    def halving_copy(part, s):
        span = pl.ds(starts[s], blocks_all >> (s + 1))
        return remote(sends[part].at[span], recvs[part].at[span], gr_send.at[part, s],
                      gr_recv.at[part, s], peer(part, s))

    def halving_start(part, s):
        size = blocks_all >> (s + 1)
        other = base(part, s) + (1 - my_bit(part, s)) * size

        @pl.loop(0, size)
        def _(i):
            sends[part][starts[s] + i] = accs[part][other + i].astype(bf16)

        halving_copy(part, s).start()

    def halving_wait(part, s):
        size = blocks_all >> (s + 1)
        mine = base(part, s) + my_bit(part, s) * size
        halving_copy(part, s).wait()

        @pl.loop(0, size)
        def _(i):
            accs[part][mine + i] += recvs[part][starts[s] + i].astype(f32)

    def put(part, g, inside, value):
        value = value.reshape(tm_size, rows, LANES)
        for j in range(tm_size):
            accs[part][block_index(orders[part], g, j), :, inside:inside + LANES] = value[j]

    per_group = group // LANES

    def put_first(at, value):
        for w in range(0, tile, LANES):
            g, r = divmod((at + w) // LANES, per_group)
            put(0, g, r * LANES, value[:, w:w + LANES])

    def put_second(at, value):
        for w in range(0, tile, LANES):
            g, r = divmod((at + w) // LANES, per_group)
            if r < per_group - 1:
                put(1, g, r * LANES, value[:, w:w + LANES])
            else:
                put(2, g, 0, value[:, w:w + LANES])

    def fin_copy(part, k):
        return remote(fins[part].at[0], fins[part].at[k], fin_send.at[part, k - 1],
                      fin_recv.at[part, k - 1], {"dp": (me_d + k) % dp_size})

    def fin_start(part):
        fins[part][0] = (accs[part][base(part, count)] * norm_scale).astype(bf16)
        for k in range(1, dp_size):
            fin_copy(part, k).start()

    def fin_wait(part):
        for k in range(1, dp_size):
            fin_copy(part, k).wait()

    def small_copy(s):
        return remote(sbuf.at[s], srecv.at[s], sm_send.at[s], sm_recv.at[s], peer(1, s))

    progress = [-1, -1, -1]

    def advance(part):
        s = progress[part]
        if s == count:
            return
        if s >= 0:
            halving_wait(part, s)
            if part == 1:
                small_copy(s).wait()
                sbuf[s + 1] = sbuf[s] + srecv[s]
        progress[part] = s + 1
        if s + 1 == count:
            fin_start(part)
            return
        halving_start(part, s + 1)
        if part == 1:
            small_copy(s + 1).start()

    pass_on(0)
    for c in range(width // tile):
        put_first(c * tile, mm(mixed[...], cot[:, c * tile:(c + 1) * tile], 0, 0))
    for c in range(width // tile):
        put_first(width + c * tile, mm(tok_t[...], dproj[:, c * tile:(c + 1) * tile]))
    advance(0)
    pass_on(1)

    @pl.loop(0, width // tile)
    def _(c):
        block_out[:, cols(c, tile)] = mm(mixed[...], wout[:, cols(c, tile)]).astype(bf16)

    advance(0)

    for h in range(2):
        for k in range(1, column):
            reduce_along(h, k).wait()

    kacc[...] = jnp.zeros_like(kacc)

    def fold(x):
        return jnp.sum(x.reshape(pooled // 8, 8, LANES), axis=0)

    @pl.loop(0, chunks)
    def _(c):
        s = c // half_chunks
        h = (c % half_chunks) // third
        here = cols(s * third + c % third)
        total = dpart[h, me_t, :, here].astype(f32) + drecv[h, 0, :, here].astype(f32)
        for k in range(1, column):
            total = total + zrecv[h, k - 1, :, here].astype(f32)
        norm = normed[:, cols(c)]
        kacc[s, 27] += fold(total * norm)
        dn = total * taps[s, pl.ds(27, 1), :]
        value = inv[:, cols(c)] * (dn - group_mean(dn) - norm * group_mean(dn * norm))
        dsum[:, cols(c)] = value
        dsum_b[:, cols(c)] = value.astype(bf16)

    second = (dsum_b, in_prev, dsum_b, in_next, 4)
    halo_start(*second)

    @pl.when(jnp.logical_not(has_prev))
    def _():
        in_prev[...] = jnp.zeros_like(in_prev)

    @pl.when(jnp.logical_not(has_next))
    def _():
        in_next[...] = jnp.zeros_like(in_next)

    halo_wait(*second)
    advance(0)

    @pl.loop(0, chunks)
    def _(c):
        s = c // half_chunks
        shifted = (
            in_next[:, cols(c)].astype(f32), dsum[:, cols(c)], in_prev[:, cols(c)].astype(f32)
        )
        for p in range(9):
            value = blocks[p * pooled:(p + 1) * pooled, cols(c)].astype(f32)
            spread = None
            for t in range(3):
                kacc[s, t * 9 + p] += fold(shifted[t] * value)
                term = shifted[t] * taps[s, pl.ds(t * 9 + p, 1), :]
                spread = term if spread is None else spread + term
            contrib[p * pooled:(p + 1) * pooled, cols(c)] = spread.astype(bf16)

    sbuf[0] = jnp.sum(kacc[...], axis=2)
    advance(0)

    for c in range(wide // tile):
        dv = mm(sel[...], contrib[:, c * tile:(c + 1) * tile], 0, 0).astype(bf16)
        dproj[:, width + c * tile:width + (c + 1) * tile] = dv
        put_second(c * tile, mm(tok_t[...], dv))

    advance(1)
    advance(2)
    advance(0)

    @pl.loop(0, width // tile)
    def _(c):
        at = pl.ds(pl.multiple_of(c * tile, tile), tile)
        grad_tok[:, cols(c, tile)] = mm(dproj[...], wqkv[at, :], 1, 1).astype(bf16)

    advance(2)
    advance(1)
    while min(progress) < count:
        advance(2)
        advance(1)
        advance(0)
    small_out[...] = sbuf[count] * norm_scale

    def write(at, value):
        if isinstance(at, tuple):
            grad_qkv[:, cols(0, LANES, at[0])] = value
            return

        @pl.when(at < width)
        def _():
            grad_out[:, cols(0, LANES, at % width)] = value

        @pl.when(at >= width)
        def _():
            grad_qkv[:, cols(0, LANES, at % width)] = value

    for part in (0, 2, 1):
        fin_wait(part)
        for k in range(dp_size):
            g = (me_d + dp_size - k) % dp_size
            for w in range(0, fins[part].shape[2], LANES):
                value = fins[part][k, :, w:w + LANES].astype(f32)
                at = g * group + w + (group - LANES if part == 2 else 0)
                write(at if part == 0 else (width + at,), value)


def shards(dp_size, tm_size, tokens, qkv_weight, pool_kernel, norm_gain, out_weight, cotangent):
    cells, width = tokens.shape[2:]
    wide = 2 * width
    orders = [stage_list(dp_size, tm_size, first) for first in (True, True, False)]
    blocks_all = dp_size * tm_size
    sel = jnp.asarray(selection(cells, cells // GRID_H), bf16)
    pooled = sel.shape[0] // 9
    rows = width // tm_size
    group = wide // dp_size
    norm_scale = float(blocks_all * cells) ** (-0.5)
    taps = jnp.concatenate([pool_kernel, norm_gain[:, None, :]], axis=1)
    taps = jnp.concatenate([taps, taps], axis=-1)
    taps_rows = taps.shape[1]
    vmem = pl.BlockSpec(memory_space=pltpu.VMEM)
    count = len(orders[0])
    column = tm_size // 2
    widths = (group, group - LANES, LANES)
    dma = pltpu.SemaphoreType.DMA
    small = (pooled, wide)
    block_out, grad_tok, grad_qkv, grad_out, total = pl.pallas_call(
        functools.partial(kernel, dp_size, tm_size, orders, norm_scale),
        out_shape=[
            jax.ShapeDtypeStruct((cells, width), bf16),
            jax.ShapeDtypeStruct((cells, width), bf16),
            jax.ShapeDtypeStruct((rows, 3 * width), f32),
            jax.ShapeDtypeStruct((rows, width), f32),
            jax.ShapeDtypeStruct((2, taps_rows, LANES), f32),
        ],
        in_specs=[vmem] * 6,
        out_specs=[vmem] * 5,
        scratch_shapes=[
            pltpu.VMEM((cells, width), bf16),
            pltpu.VMEM((9 * pooled, wide), bf16),
            pltpu.VMEM((cells, width), bf16),
            pltpu.VMEM((cells, width), bf16),
            pltpu.VMEM((cells, 3 * width), bf16),
            pltpu.VMEM((tm_size, pooled, wide), bf16),
            pltpu.VMEM((2, tm_size, pooled, width), bf16),
            pltpu.VMEM((2, column, pooled, width), bf16),
            pltpu.VMEM((2, column - 1, pooled, width), bf16),
            pltpu.VMEM((2, column - 1, pooled, width), bf16),
        ]
        + [pltpu.VMEM(small, f32)] * 8
        + [pltpu.VMEM(small, bf16)] * 3
        + [
            pltpu.VMEM((9 * pooled, wide), bf16),
            pltpu.VMEM((width, cells), bf16),
        ]
        + [pltpu.VMEM((blocks_all, rows, w), f32) for w in widths]
        + [pltpu.VMEM((blocks_all, rows, w), bf16) for w in widths * 2]
        + [pltpu.VMEM((dp_size, rows, w), bf16) for w in widths]
        + [
            pltpu.VMEM((2, taps_rows, 8, LANES), f32),
            pltpu.VMEM((count + 1, 2, taps_rows, LANES), f32),
            pltpu.VMEM((count, 2, taps_rows, LANES), f32),
            dma((6,)),
            dma((6,)),
            dma((2, column)),
            dma((2, column)),
            dma((2, column)),
            dma((2, column)),
            dma((2, column - 1)),
            dma((2, column - 1)),
            dma((3, count)),
            dma((3, count)),
            dma((count,)),
            dma((count,)),
            dma((3, dp_size - 1)),
            dma((3, dp_size - 1)),
        ],
        compiler_params=pltpu.CompilerParams(
            collective_id=0, has_side_effects=True, vmem_limit_bytes=63 * 1024 * 1024
        ),
        cost_estimate=pl.CostEstimate(
            flops=10 * 10**9, bytes_accessed=10 * 10**6, transcendentals=0
        ),
    )(
        tokens.reshape(cells, width), qkv_weight, taps, out_weight,
        cotangent.reshape(cells, width), sel,
    )
    head = width // HEADS
    summed = total[:, :, :head] + total[:, :, head:]
    return (
        block_out.reshape(tokens.shape), grad_tok.reshape(tokens.shape), grad_qkv, grad_out,
        summed[:, :-1], summed[:, -1],
    )


def solution(mesh):
    placed = (P("dp", "tm", None, None), P(), P(), P(), P(), P("dp", "tm", None, None))
    return jax.shard_map(
        functools.partial(shards, mesh.shape["dp"], mesh.shape["tm"]),
        mesh=mesh,
        in_specs=placed,
        out_specs=(
            P("dp", "tm", None, None),
            P("dp", "tm", None, None),
            P("tm", None),
            P("tm", None),
            P(),
            P(),
        ),
        check_vma=False,
    )
```
